128 devices in a mesh: col: 8 (over y_lo, x), dev: 8 (over y_hi, z), ao: 2 (over core).
Axes of the slice: x: 4, y: 4 (y_hi: 2, y_lo: 2; y = y_hi * 2 + y_lo), z: 4, core: 2. Of those that a mesh axis runs over, the one named last changes fastest.
Arguments:
- raw_ints: bfloat16 [1024, 32, 512], P('dev', None, 'col'), may hold values from -1.078125 to 1.078125
- metric: bfloat16 [1024, 1024], P('dev'), may hold values from -0.1875 to 0.1875
- amplitudes: bfloat16 [512, 512, 2048], P('col', 'dev', 'ao'), may hold values from -0.017944336 to 0.017944336
- pair_list: int32 [2, 2048], P(None, 'ao'), may hold values from 0 to 63
- occ_energy: float32 [64], replicated, may hold values from -2 to -0.3
- vir_energy: float32 [512], replicated, may hold values from 0.2 to 3
- window_ids: int32 [32], replicated, may hold values from 0 to 511, as said below
Outputs:
- residual: float32 [1024, 2048], P(('col', 'dev'), 'ao')
The draws below stay inside these ranges and needn't reach their ends.
Inputs may be any that keep to these rules, and one draw needn't show every extreme that they name: `window_ids`: distinct virtual orbitals; 0 and 511 are always among them.
All inputs are finite; a program needn't handle non-finite values.
Results may differ from the reference program's by a relative error of at most 0.0041.
Values may be sent and summed in bfloat16 or wider, within the bound.
A program may use at most 128 MiB of HBM per device.

```python
import jax
import jax.numpy as jnp
from jax import lax

NV = 512
NAUX = 1024
NOCC = 64
W = 32
NPAIRS = 2048


def draw_window_ids(key, part):
    middle_ids = jax.random.permutation(key, NV - 2)[:W - 2] + 1
    combined = jnp.concatenate([jnp.array([0, NV - 1], dtype=jnp.int32), middle_ids.astype(jnp.int32)])
    return jax.random.permutation(jax.random.fold_in(key, 7), combined).astype(jnp.int32)


def set_ends(result, stream_key, least, high):
    dims = result.shape
    place = [jax.random.randint(jax.random.fold_in(stream_key, axis), (), 0, dims[axis]) for axis in range(len(dims))]
    result = result.at[tuple(place)].set(least)
    longest = dims.index(max(dims))
    place[longest] = (place[longest] + 1) % dims[longest]
    return result.at[tuple(place)].set(high)


def shard_levels(stream_key, extent, split, smallest, high):
    gain, own = 1.0, jax.random.fold_in(stream_key, 6)
    for axis_at, shards_of in split:
        steps = jnp.exp(jax.random.uniform(jax.random.fold_in(own, axis_at), (shards_of,), jnp.float32, smallest / len(split), high / len(split)))
        gain = gain * jnp.repeat(steps, extent[axis_at] // shards_of).reshape([-1 if axis == axis_at else 1 for axis in range(len(extent))])
    return gain


def bell_draw(key, extent, scale, reach, cuts=(), kind=jnp.bfloat16):
    gain = shard_levels(key, extent, cuts, -0.22, 0.18) if cuts else 1.0
    values = jax.random.normal(key, extent, jnp.float32) * scale * gain
    return jnp.minimum(jnp.maximum(values, -reach), reach).astype(kind)


def setup_inputs(seed: int = 0) -> dict:
    keys = jax.random.split(jax.random.key(seed), 8)
    raw_ints = bell_draw(keys[0], (NAUX, W, NV), 0.18, 1.078125, ((0, 8), (2, 8)))
    metric = bell_draw(keys[1], (NAUX, NAUX), NAUX ** -0.5, 0.1875, ((0, 8),))
    amplitudes = bell_draw(keys[2], (NV, NV, NPAIRS), 0.003, 0.017944336, ((0, 8), (1, 8), (2, 2)))
    pair_list = set_ends(jax.random.randint(keys[3], (2, NPAIRS), 0, NOCC), jax.random.fold_in(keys[3], 1), 0, NOCC - 1).astype(jnp.int32)
    occ_energy = jnp.clip(jax.random.uniform(keys[4], (NOCC,), jnp.float32, -2.0, -0.3), -2.0, -0.3)
    vir_energy = jnp.clip(jax.random.uniform(keys[5], (NV,), jnp.float32, 0.2, 3.0), 0.2, 3.0)
    window_ids = draw_window_ids(jax.random.fold_in(keys[7], 71), 0)
    return dict(raw_ints=raw_ints, metric=metric, amplitudes=amplitudes, pair_list=pair_list, occ_energy=occ_energy, vir_energy=vir_energy, window_ids=window_ids)


def reference(raw_ints, metric, amplitudes, pair_list, occ_energy, vir_energy, window_ids):
    flat_factors = jnp.dot(metric, raw_ints.reshape(NAUX, W * NV), preferred_element_type=jnp.float32).astype(jnp.bfloat16)
    cube = flat_factors.reshape(NAUX, W, NV)
    amp_matrix = amplitudes.reshape(NV * NV, NPAIRS)

    def ladder_row(column):
        right_side = lax.dynamic_index_in_dim(cube, column, 1, keepdims=False)
        integrals = lax.dot_general(flat_factors, right_side, (((0,), (0,)), ((), ())), preferred_element_type=jnp.float32)
        integrals = integrals.astype(jnp.bfloat16).reshape(W, NV * NV)
        return jnp.dot(integrals, amp_matrix, preferred_element_type=jnp.float32)

    stacked = lax.map(ladder_row, jnp.arange(W, dtype=jnp.int32))
    summed = jnp.transpose(stacked, (1, 0, 2)).reshape(W * W, NPAIRS)
    energy_i = occ_energy[pair_list[0]]
    energy_j = occ_energy[pair_list[1]]
    window_energy = vir_energy[window_ids]
    energy_first = jnp.repeat(window_energy, W)
    energy_second = jnp.tile(window_energy, W)
    denominator = (energy_i + energy_j)[None, :] - (energy_first + energy_second)[:, None]
    return summed / denominator
```

```python
import jax
import jax.numpy as jnp
from jax import lax
from jax.experimental import pallas as pl
from jax.experimental.pallas import tpu as pltpu
from jax.sharding import PartitionSpec as P

MESH = pl.DeviceIdType.MESH
F32, BF16 = jnp.float32, jnp.bfloat16
NT = (((1,), (1,)), ((), ()))

PARTNER, MINUS, PLUS, MINUS_P, PLUS_P, FAR_A, FAR_AP, FAR_B, FAR_BP = range(9)
SWAP = 9


def select_energy(positions, table):
    labels = jnp.arange(table.shape[0], dtype=jnp.int32)
    return jnp.sum(jnp.where(positions[:, None] == labels[None, :], table[None, :], 0.0), axis=1)


def ladder_kernel(
    raw_ca, raw_bd, met, amp, out,
    work, mbuf, acc_l, acc_r, fac_l, fac_r, amps, sums, send1, land1, send2, land2,
    local_sem, ag_send, ag_recv, rel_send, rel_recv, rs_send, rs_recv,
):
    i, j, o = lax.axis_index("col"), lax.axis_index("dev"), lax.axis_index("ao")
    flip = lambda g: lax.rem(g + 4, 8)
    ring = lambda g, step: (g // 4) * 4 + lax.rem(lax.rem(g, 4) + step, 4)
    along_dev = lambda g: (i, g, o)
    along_col = lambda g: (g, j, o)
    sibling = (i, j, 1 - o)
    swap = (j, i, o)

    barrier = pltpu.get_barrier_semaphore()

    def greet(device):
        pl.semaphore_signal(barrier, inc=1, device_id=device, device_id_type=MESH)

    for d in range(1, 8):
        greet(along_dev(lax.rem(j + d, 8)))
        greet(along_col(lax.rem(i + d, 8)))
    greet(sibling)
    greet((flip(i), flip(j), o))

    @pl.when(i != j)
    def _():
        greet(swap)

    pl.semaphore_wait(barrier, 16 + jnp.where(i != j, 1, 0))

    pending = []

    def push(src, dst, send_sem, recv_sem, device):
        copy = pltpu.make_async_remote_copy(
            src_ref=src, dst_ref=dst, send_sem=send_sem, recv_sem=recv_sem,
            device_id=device, device_id_type=MESH,
        )
        copy.start()
        pending.append(copy)

    def landed(dst, recv_sem):
        pltpu.make_async_remote_copy(
            src_ref=dst, dst_ref=dst, send_sem=recv_sem, recv_sem=recv_sem,
            device_id=sibling, device_id_type=MESH,
        ).wait_recv()

    class Gather:
        def __init__(self, which, me, to, partner, half, part):
            self.which, self.me, self.half, self.part = which, me, half, part
            self.up, self.down = to(ring(me, 1)), to(ring(me, 3))
            self.partner = partner
            plus, minus, far = ring(me, 1), ring(me, 3), ring(me, 2)
            self.plus, self.minus, self.far = plus, minus, far
            self.place = {
                PARTNER: (flip(me), None), MINUS: (minus, None), PLUS: (plus, None),
                MINUS_P: (flip(minus), None), PLUS_P: (flip(plus), None),
                FAR_A: (far, 0), FAR_AP: (flip(far), 0), FAR_B: (far, 1), FAR_BP: (flip(far), 1),
            }

        def spot(self, kind, core):
            piece, quarter = self.place[kind]
            if quarter is None:
                return self.half(piece, core)
            return self.part(piece, core, quarter)

        def send(self, src, dst, kind, device):
            push(src, dst, ag_send.at[self.which, kind], ag_recv.at[self.which, kind], device)

        def send_own(self, src):
            dst = self.half(self.me, o)
            self.send(src, dst, MINUS, self.up)
            self.send(src, dst, PLUS, self.down)
            self.send(src, dst, PARTNER, self.partner)

        def arrive(self, *kinds):
            for kind in kinds:
                spot = self.spot(kind, o)
                landed(spot, ag_recv.at[self.which, kind])
                if kind == PARTNER:
                    self.send(spot, spot, MINUS_P, self.up)
                    self.send(spot, spot, PLUS_P, self.down)
                elif kind in (MINUS, MINUS_P):
                    piece = self.part(self.place[kind][0], o, 0)
                    self.send(piece, piece, FAR_A if kind == MINUS else FAR_AP, self.up)
                elif kind in (PLUS, PLUS_P):
                    piece = self.part(self.place[kind][0], o, 1)
                    self.send(piece, piece, FAR_B if kind == PLUS else FAR_BP, self.down)
                push(spot, spot, rel_send.at[self.which, kind], rel_recv.at[self.which, kind], sibling)

        def from_sibling(self, *kinds):
            for kind in kinds:
                landed(self.spot(kind, 1 - o), rel_recv.at[self.which, kind])

    left = Gather(
        0, j, along_dev, along_dev(flip(j)),
        lambda k, core: work.at[2 * k + core],
        lambda k, core, q: work.at[2 * k + core, pl.ds(512 * q, 512)],
    )
    right = Gather(
        1, i, along_col, along_col(flip(i)),
        lambda k, core: work.at[16 + 2 * k + core],
        lambda k, core, q: work.at[16 + 2 * k + core, pl.ds(512 * q, 512)],
    )
    fit = Gather(
        2, j, along_dev, (flip(i), flip(j), o),
        lambda k, core: mbuf.at[k, pl.ds(pl.multiple_of(64 * core, 64), 64)],
        lambda k, core, q: mbuf.at[k, pl.ds(pl.multiple_of(64 * core + 32 * q, 32), 32)],
    )

    own_half = pl.ds(pl.multiple_of(1024 * o, 1024), 1024)
    swap_dst = work.at[16 + 2 * j + o]
    swap_src = raw_bd.at[own_half]
    swap_here = work.at[16 + 2 * i + o]

    fit.send_own(met.at[pl.ds(pl.multiple_of(64 * o, 64), 64)])
    left.send_own(raw_ca.at[own_half])
    swap_copy = pltpu.make_async_remote_copy(
        src_ref=swap_src, dst_ref=swap_dst, send_sem=ag_send.at[1, SWAP],
        recv_sem=ag_recv.at[1, SWAP], device_id=swap, device_id_type=MESH,
    )

    @pl.when(i != j)
    def _():
        swap_copy.start()

    @pl.when(i == j)
    def _():
        here = pltpu.make_async_copy(swap_src, swap_here, local_sem.at[3])
        here.start()
        here.wait()

    own_l = [
        pltpu.make_async_copy(raw_ca.at[pl.ds(1024 * h, 1024)], work.at[2 * j + h], local_sem.at[4 + h])
        for h in range(2)
    ]
    own_m = pltpu.make_async_copy(met, mbuf.at[j], local_sem.at[1])
    get_amps = pltpu.make_async_copy(amp, amps, local_sem.at[2])
    for copy in own_l + [own_m, get_amps]:
        copy.start()

    fit.arrive(PARTNER)
    left.arrive(PARTNER)

    @pl.when(i != j)
    def _():
        landed(swap_here, ag_recv.at[1, SWAP])

    right.send_own(swap_here)
    push(swap_here, swap_here, rel_send.at[1, SWAP], rel_recv.at[1, SWAP], sibling)
    fit.arrive(MINUS, PLUS, MINUS_P, PLUS_P)
    left.arrive(MINUS, PLUS)
    right.arrive(PARTNER)
    left.arrive(MINUS_P, PLUS_P)
    fit.arrive(FAR_A, FAR_B, FAR_AP, FAR_BP)
    for copy in own_l + [own_m]:
        copy.wait()
    fit.from_sibling(*range(9))

    def m_slice(k):
        return mbuf[:, :, pl.ds(pl.multiple_of(k * 128, 128), 128)].reshape(1024, 128)

    def fit_left(k, first=False, last=False):
        two = flip(k)
        m = jnp.concatenate([m_slice(k), m_slice(two)], axis=1)

        def body(n, _):
            h, at = n // 2, pl.multiple_of(lax.rem(n, 2) * 512, 512)
            rows = pl.ds(pl.multiple_of(n * 512, 512), 512)
            x = jnp.concatenate([work[2 * k + h, pl.ds(at, 512), :], work[2 * two + h, pl.ds(at, 512), :]], axis=1)
            y = lax.dot_general(x, m, NT, preferred_element_type=F32)
            if not first:
                y = y + acc_l[rows, :]
            if last:
                fac_l[rows, :] = y.astype(BF16)
            else:
                acc_l[rows, :] = y
            return 0

        lax.fori_loop(0, 4, body, 0)

    def fit_right(k, first=False, last=False):
        two = flip(k)
        m = jnp.concatenate([m_slice(k), m_slice(two)], axis=1)

        def body(n, _):
            h, at = n // 2, pl.multiple_of(lax.rem(n, 2) * 512, 512)
            cols = pl.ds(pl.multiple_of(n * 512, 512), 512)
            x = jnp.concatenate(
                [work[16 + 2 * k + h, pl.ds(at, 512), :], work[16 + 2 * two + h, pl.ds(at, 512), :]], axis=1)
            y = lax.dot_general(m, x, NT, preferred_element_type=F32)
            if not first:
                y = y + acc_r[:, cols]
            if last:
                fac_r[:, cols] = y.astype(BF16)
            else:
                acc_r[:, cols] = y
            return 0

        lax.fori_loop(0, 4, body, 0)

    left.from_sibling(PARTNER)
    fit_left(left.me, first=True)
    right.arrive(MINUS, PLUS)
    left.from_sibling(MINUS, MINUS_P)
    fit_left(left.minus)
    right.arrive(MINUS_P, PLUS_P)
    left.from_sibling(PLUS, PLUS_P)
    fit_left(left.plus)
    left.arrive(FAR_A, FAR_B, FAR_AP, FAR_BP)
    landed(work.at[16 + 2 * i + 1 - o], rel_recv.at[1, SWAP])
    right.from_sibling(PARTNER)
    fit_right(right.me, first=True)
    right.from_sibling(MINUS, MINUS_P)
    fit_right(right.minus)
    right.from_sibling(PLUS, PLUS_P)
    fit_right(right.plus)
    left.from_sibling(FAR_A, FAR_B, FAR_AP, FAR_BP)
    fit_left(left.far, last=True)
    right.arrive(FAR_A, FAR_B, FAR_AP, FAR_BP)
    right.from_sibling(FAR_A, FAR_B, FAR_AP, FAR_BP)
    fit_right(right.far, last=True)

    for copy in pending:
        copy.wait_send()
    pending.clear()

    @pl.when(i != j)
    def _():
        swap_copy.wait_send()

    def ladder_tile(n, _):
        rc, lc = n // 4, lax.rem(n, 4)
        rows = pl.ds(pl.multiple_of(rc * 512, 512), 512)
        cols = pl.ds(pl.multiple_of(lc * 512, 512), 512)
        x = jnp.dot(fac_l[rows, :], fac_r[:, cols], preferred_element_type=F32).astype(BF16)
        x = x.reshape(8, 2, 32, 512)
        even, odd = x[:, 0], x[:, 1]
        for v in range(8):
            lanes = slice(64 * v, 64 * v + 64)
            y = jnp.concatenate([even[:, :, lanes], odd[:, :, lanes]], axis=2)
            at = pl.multiple_of(lc * 256 + v * 32, 32)
            work[pl.ds(rc * 8, 8), pl.ds(at, 32), :] = y
        return 0

    lax.fori_loop(0, 16, ladder_tile, 0)
    get_amps.wait()

    axes = [(i, along_col, j, along_dev), (j, along_dev, i, along_col)]
    for q in range(4):
        pcols = slice(256 * q, 256 * q + 256)

        def sum_rows(n, _):
            rows = pl.ds(pl.multiple_of(n * 512, 512), 512)
            total = None
            for kc in range(4):
                x = jnp.concatenate([work[8 * kc + c, rows, :] for c in range(8)], axis=1)
                y = jnp.dot(x, amps[1024 * kc:1024 * kc + 1024, pcols], preferred_element_type=F32)
                total = y if total is None else total + y
            for half in range(2):
                sums[half, rows, :] = total[:, 128 * half:128 * half + 128]
            return 0

        lax.fori_loop(0, 2, sum_rows, 0)
        me, to, _, _ = axes[q % 2]
        for a in range(32):
            x = jnp.concatenate([sums[half, pl.ds(a, 32, stride=32), :] for half in range(2)], axis=1).astype(BF16)
            if q % 2 == 0:
                send1[q, a // 4, 32 * (a % 4):32 * (a % 4) + 32, :] = x
            else:
                for h in range(2):
                    send1[q, 2 * (a % 4) + h, 16 * (a // 4):16 * (a // 4) + 16, :] = x[16 * h:16 * h + 16]
        for d in range(1, 8):
            peer = lax.rem(me + d, 8)
            push(send1.at[q, peer], land1.at[q, me], rs_send.at[0, q, d], rs_recv.at[0, q, d], to(peer))

    for q in range(4):
        me, _, other, to = axes[q % 2]
        total = send1[q, me].astype(F32)
        for d in range(1, 8):
            src = lax.rem(me + 8 - d, 8)
            landed(land1.at[q, src], rs_recv.at[0, q, d])
            total = total + land1[q, src].astype(F32)
        send2[q] = total.astype(BF16).reshape(8, 16, 256)
        for d in range(1, 8):
            peer = lax.rem(other + d, 8)
            push(send2.at[q, peer], land2.at[q, other], rs_send.at[1, q, d], rs_recv.at[1, q, d], to(peer))

    for q in range(4):
        _, _, other, to = axes[q % 2]
        total = send2[q, other].astype(F32)
        for d in range(1, 8):
            src = lax.rem(other + 8 - d, 8)
            landed(land2.at[q, src], rs_recv.at[1, q, d])
            total = total + land2[q, src].astype(F32)
        out[:, 256 * q:256 * q + 256] = total

    for copy in pending:
        copy.wait_send()


def on_device(raw_ints, metric, amplitudes, pair_list, occ_energy, vir_energy, window_ids):
    width = raw_ints.shape[1]
    raw_ca = jnp.transpose(raw_ints, (2, 1, 0)).reshape(2048, 128)
    raw_bd = jnp.transpose(raw_ints, (1, 2, 0)).reshape(2048, 128)
    amp = amplitudes.reshape(4096, 1024)
    vmem = lambda shape, kind: pltpu.VMEM(shape, kind)
    dma = pltpu.SemaphoreType.DMA
    summed = pl.pallas_call(
        ladder_kernel,
        out_shape=jax.ShapeDtypeStruct((16, 1024), F32),
        in_specs=[pl.BlockSpec(memory_space=pl.ANY)] * 4,
        out_specs=pl.BlockSpec(memory_space=pltpu.VMEM),
        scratch_shapes=[
            vmem((32, 1024, 128), BF16),
            vmem((8, 128, 1024), BF16),
            vmem((2048, 1024), F32),
            vmem((1024, 2048), F32),
            vmem((2048, 1024), BF16),
            vmem((1024, 2048), BF16),
            vmem((4096, 1024), BF16),
            vmem((2, 1024, 128), F32),
            vmem((4, 8, 128, 256), BF16),
            vmem((4, 8, 128, 256), BF16),
            vmem((4, 8, 16, 256), BF16),
            vmem((4, 8, 16, 256), BF16),
            dma((6,)),
            dma((3, 10)), dma((3, 10)), dma((3, 10)), dma((3, 10)),
            dma((2, 4, 8)), dma((2, 4, 8)),
        ],
        compiler_params=pltpu.CompilerParams(
            collective_id=0, has_side_effects=True, vmem_limit_bytes=60 * 2**20
        ),
        cost_estimate=pl.CostEstimate(flops=26 * 10**9, bytes_accessed=10 * 10**6, transcendentals=0),
    )(raw_ca, raw_bd, metric, amp)
    row_total = summed.shape[0]
    global_rows = lax.axis_index(("col", "dev")) * row_total + jnp.arange(row_total, dtype=jnp.int32)
    window_energy = select_energy(window_ids, vir_energy)
    energy_first = select_energy(global_rows // width, window_energy)
    energy_second = select_energy(global_rows % width, window_energy)
    energy_i = select_energy(pair_list[0], occ_energy)
    energy_j = select_energy(pair_list[1], occ_energy)
    denominator = (energy_i + energy_j)[None, :] - (energy_first + energy_second)[:, None]
    return summed / denominator


def solution(mesh):
    in_specs = (
        P("dev", None, "col"),
        P("dev", None),
        P("col", "dev", "ao"),
        P(None, "ao"),
        P(),
        P(),
        P(),
    )
    out_specs = P(("col", "dev"), "ao")
    return jax.shard_map(
        on_device, mesh=mesh, in_specs=in_specs, out_specs=out_specs, check_vma=False
    )
```

```python
import jax
import jax.numpy as jnp
from jax import lax
from jax.experimental import pallas as pl
from jax.experimental.pallas import tpu as pltpu
from jax.sharding import PartitionSpec as P

MESH = pl.DeviceIdType.MESH
F32, BF16 = jnp.float32, jnp.bfloat16
NT = (((1,), (1,)), ((), ()))

PARTNER, MINUS, PLUS, MINUS_P, PLUS_P, FAR_A, FAR_AP, FAR_B, FAR_BP = range(9)
OWN = 9


def select_energy(positions, table):
    labels = jnp.arange(table.shape[0], dtype=jnp.int32)
    return jnp.sum(jnp.where(positions[:, None] == labels[None, :], table[None, :], 0.0), axis=1)


def ladder_kernel(
    raw_ca, raw_bd, met, amp, out,
    work, mbuf, acc_l, fac_l, fac_r, amps, sums, send1, land1, send2, land2,
    local_sem, deal_send, deal_recv, ag_send, ag_recv, rel_send, rel_recv, rs_send, rs_recv,
):
    i, j, o = lax.axis_index("col"), lax.axis_index("dev"), lax.axis_index("ao")
    flip = lambda g: lax.rem(g + 4, 8)
    ring = lambda g, step: (g // 4) * 4 + lax.rem(lax.rem(g, 4) + step, 4)
    along_dev = lambda g: (i, g, o)
    along_col = lambda g: (g, j, o)
    sibling = (i, j, 1 - o)
    u, v = lax.rem(i // 4 + j // 4, 2) * 4 + lax.rem(i, 4), j
    at = lambda u, v: (lax.rem(u // 4 + v // 4, 2) * 4 + lax.rem(u, 4), v, o)

    barrier = pltpu.get_barrier_semaphore()

    def greet(device):
        pl.semaphore_signal(barrier, inc=1, device_id=device, device_id_type=MESH)

    for d in (1, 3):
        greet(along_col(ring(i, d)))
        greet(along_dev(ring(j, d)))
    greet(along_col(flip(i)))
    greet(along_dev(flip(j)))
    greet((flip(i), flip(j), o))
    greet(sibling)
    diagonal = i == j
    for k in range(8):
        @pl.when(jnp.logical_not(diagonal & (j == k)))
        def _():
            greet((j, k, o))

    sums[...] = jnp.zeros_like(sums)
    pl.semaphore_wait(barrier, 16 - jnp.where(diagonal, 1, 0))

    pending = []

    def push(src, dst, send_sem, recv_sem, device):
        copy = pltpu.make_async_remote_copy(
            src_ref=src, dst_ref=dst, send_sem=send_sem, recv_sem=recv_sem,
            device_id=device, device_id_type=MESH,
        )
        copy.start()
        pending.append(copy)

    def landed(dst, recv_sem):
        pltpu.make_async_remote_copy(
            src_ref=dst, dst_ref=dst, send_sem=recv_sem, recv_sem=recv_sem,
            device_id=sibling, device_id_type=MESH,
        ).wait_recv()

    class Gather:
        def __init__(self, which, me, to, partner, half, part):
            self.which, self.me, self.half, self.part = which, me, half, part
            self.up, self.down = to(ring(me, 1)), to(ring(me, 3))
            self.partner = partner
            plus, minus, far = ring(me, 1), ring(me, 3), ring(me, 2)
            self.plus, self.minus, self.far = plus, minus, far
            self.place = {
                PARTNER: (flip(me), None), MINUS: (minus, None), PLUS: (plus, None),
                MINUS_P: (flip(minus), None), PLUS_P: (flip(plus), None),
                FAR_A: (far, 0), FAR_AP: (flip(far), 0), FAR_B: (far, 1), FAR_BP: (flip(far), 1),
            }

        def spot(self, kind, core):
            piece, quarter = self.place[kind]
            if quarter is None:
                return self.half(piece, core)
            return self.part(piece, core, quarter)

        def send(self, src, dst, kind, device):
            push(src, dst, ag_send.at[self.which, kind], ag_recv.at[self.which, kind], device)

        def send_own(self, src):
            dst = self.half(self.me, o)
            self.send(src, dst, MINUS, self.up)
            self.send(src, dst, PLUS, self.down)
            self.send(src, dst, PARTNER, self.partner)

        def arrive(self, *kinds):
            for kind in kinds:
                spot = self.spot(kind, o)
                landed(spot, ag_recv.at[self.which, kind])
                piece = self.place[kind][0]
                if self.which == 2 and kind in (MINUS, PLUS, FAR_A, FAR_B):
                    self.send(spot, spot, {MINUS: MINUS_P, PLUS: PLUS_P, FAR_A: FAR_AP, FAR_B: FAR_BP}[kind], self.partner)
                if self.which != 2 and kind == PARTNER:
                    self.send(spot, spot, MINUS_P, self.up)
                    self.send(spot, spot, PLUS_P, self.down)
                elif kind == MINUS or self.which != 2 and kind == MINUS_P:
                    first = self.part(piece, o, 0)
                    self.send(first, first, FAR_A if kind == MINUS else FAR_AP, self.up)
                elif kind == PLUS or self.which != 2 and kind == PLUS_P:
                    second = self.part(piece, o, 1)
                    self.send(second, second, FAR_B if kind == PLUS else FAR_BP, self.down)
                push(spot, spot, rel_send.at[self.which, kind], rel_recv.at[self.which, kind], sibling)

        def from_sibling(self, *kinds):
            for kind in kinds:
                landed(self.spot(kind, 1 - o), rel_recv.at[self.which, kind])

    left = Gather(
        0, j, along_dev, along_dev(flip(j)),
        lambda k, core: work.at[2 * k + core],
        lambda k, core, q: work.at[2 * k + core, pl.ds(512 * q, 512)],
    )
    right = Gather(
        1, i, along_col, along_col(flip(i)),
        lambda k, core: work.at[16 + 2 * k + core],
        lambda k, core, q: work.at[16 + 2 * k + core, pl.ds(512 * q, 512)],
    )
    fit = Gather(
        2, j, along_dev, (flip(i), flip(j), o),
        lambda k, core: mbuf.at[k, pl.ds(pl.multiple_of(64 * core, 64), 64)],
        lambda k, core, q: mbuf.at[k, pl.ds(pl.multiple_of(64 * core + 32 * q, 32), 32)],
    )

    own_half = pl.ds(pl.multiple_of(1024 * o, 1024), 1024)
    fit.send_own(met.at[pl.ds(pl.multiple_of(64 * o, 64), 64)])
    chunk = lambda g: raw_bd.at[pl.ds(pl.multiple_of(256 * g + 128 * o, 128), 128)]
    chunk_at = lambda g, k: work.at[16 + 2 * g + o, pl.ds(pl.multiple_of(128 * k, 128), 128)]
    for d in range(8):
        g = lax.rem(i + d, 8)

        @pl.when(jnp.logical_not(diagonal & (g == i)))
        def _():
            pltpu.make_async_remote_copy(
                src_ref=chunk(g), dst_ref=chunk_at(g, j), send_sem=deal_send.at[g],
                recv_sem=deal_recv.at[j], device_id=(g, i, o), device_id_type=MESH,
            ).start()

    @pl.when(diagonal)
    def _():
        here = pltpu.make_async_copy(chunk(i), chunk_at(i, j), local_sem.at[3])
        here.start()
        here.wait()

    left.send_own(raw_ca.at[own_half])

    own_l = [
        pltpu.make_async_copy(raw_ca.at[pl.ds(1024 * h, 1024)], work.at[2 * j + h], local_sem.at[4 + h])
        for h in range(2)
    ]
    own_m = pltpu.make_async_copy(met, mbuf.at[j], local_sem.at[1])
    get_amps = pltpu.make_async_copy(amp, amps, local_sem.at[2])
    for copy in own_l + [own_m, get_amps]:
        copy.start()

    fit.arrive(PARTNER)
    left.arrive(PARTNER)

    for k in range(8):
        @pl.when(jnp.logical_not(diagonal & (j == k)))
        def _():
            landed(chunk_at(i, k), deal_recv.at[k])

    own_chunk = work.at[16 + 2 * i + o]
    right.send_own(own_chunk)
    push(own_chunk, own_chunk, rel_send.at[1, OWN], rel_recv.at[1, OWN], sibling)
    fit.arrive(MINUS, PLUS)
    left.arrive(MINUS, PLUS)
    fit.arrive(FAR_A, FAR_B)
    right.arrive(PARTNER)
    fit.arrive(MINUS_P, PLUS_P)
    left.arrive(MINUS_P, PLUS_P)
    right.arrive(MINUS, PLUS)
    fit.arrive(FAR_AP, FAR_BP)
    for copy in own_l + [own_m]:
        copy.wait()
    fit.from_sibling(*range(9))

    def m_slice(k):
        return mbuf[:, :, pl.ds(pl.multiple_of(k * 128, 128), 128)].reshape(1024, 128)

    def fit_left(pieces, first=False, last=False):
        m = jnp.concatenate([m_slice(k) for k in pieces], axis=1)

        def body(n, _):
            rows = pl.ds(pl.multiple_of(n * 1024, 1024), 1024)
            x = jnp.concatenate([work[2 * k + n] for k in pieces], axis=1)
            y = lax.dot_general(x, m, NT, preferred_element_type=F32)
            if not first:
                y = y + acc_l[rows, :]
            if last:
                fac_l[rows, :] = y.astype(BF16)
            else:
                acc_l[rows, :] = y
            return 0

        lax.fori_loop(0, 2, body, 0)

    def fit_right(count, piece_of):
        def body(n, _):
            one = piece_of(n)
            two = flip(one)
            x = jnp.concatenate([
                jnp.concatenate([work[16 + 2 * g + h, 128 * k:128 * k + 128, :] for k in range(8)], axis=1)
                for g in (one, two) for h in range(2)
            ], axis=0)
            y = lax.dot_general(mbuf[...].reshape(1024, 1024), x, NT, preferred_element_type=F32).astype(BF16)
            fac_r[:, pl.ds(pl.multiple_of(256 * one, 256), 256)] = y[:, :256]
            fac_r[:, pl.ds(pl.multiple_of(256 * two, 256), 256)] = y[:, 256:]
            return 0

        lax.fori_loop(0, count, body, 0)

    left.from_sibling(PARTNER)
    fit_left([left.me, flip(left.me)], first=True)
    right.arrive(MINUS_P, PLUS_P)
    landed(work.at[16 + 2 * i + 1 - o], rel_recv.at[1, OWN])
    right.from_sibling(PARTNER)
    fit_right(1, lambda n: i)
    left.from_sibling(MINUS, MINUS_P, PLUS, PLUS_P)
    fit_left([left.minus, flip(left.minus), left.plus, flip(left.plus)])
    left.arrive(FAR_A, FAR_B, FAR_AP, FAR_BP)
    right.from_sibling(MINUS, MINUS_P, PLUS, PLUS_P)
    fit_right(2, lambda n: ring(i, 1 + 2 * n))
    right.arrive(FAR_A, FAR_B, FAR_AP, FAR_BP)
    left.from_sibling(FAR_A, FAR_B, FAR_AP, FAR_BP)
    fit_left([left.far, flip(left.far)], last=True)
    right.from_sibling(FAR_A, FAR_B, FAR_AP, FAR_BP)
    fit_right(1, lambda n: right.far)

    for copy in pending:
        copy.wait_send()
    pending.clear()

    for g in range(8):
        @pl.when(jnp.logical_not(diagonal & (g == i)))
        def _():
            pltpu.make_async_remote_copy(
                src_ref=chunk(g), dst_ref=chunk_at(g, j), send_sem=deal_send.at[g],
                recv_sem=deal_recv.at[j], device_id=(g, i, o), device_id_type=MESH,
            ).wait_send()

    def ladder_tile(n, _):
        rc, lc = n // 2, lax.rem(n, 2)
        rows = pl.ds(pl.multiple_of(rc * 512, 512), 512)
        cols = pl.ds(pl.multiple_of(lc * 1024, 1024), 1024)
        x = jnp.dot(fac_l[rows, :], fac_r[:, cols], preferred_element_type=F32).astype(BF16)
        x = x.reshape(8, 2, 32, 1024)
        even, odd = x[:, 0], x[:, 1]
        for v in range(16):
            lanes = slice(64 * v, 64 * v + 64)
            y = jnp.concatenate([even[:, :, lanes], odd[:, :, lanes]], axis=2)
            at = pl.multiple_of(lc * 512 + v * 32, 32)
            work[pl.ds(rc * 8, 8), pl.ds(at, 32), :] = y
        return 0

    lax.fori_loop(0, 8, ladder_tile, 0)
    get_amps.wait()

    def route(stage, c):
        if (c + stage) % 2 == 0:
            return u, lambda g: at(g, v)
        return v, lambda g: at(u, g)

    def spread(stage, c, src, dst):
        me, to = route(stage, c)
        for d in (1, 7, 4, 3, 5, 2, 6):
            peer = lax.rem(me + d, 8)
            push(src.at[c, peer], dst.at[c, d - 1], rs_send.at[stage, c, d - 1], rs_recv.at[stage, c, d - 1], to(peer))

    def collect(stage, c, src, dst):
        total = src[c, route(stage, c)[0]].astype(F32)
        for d in range(7):
            landed(dst.at[c, d], rs_recv.at[stage, c, d])
            total = total + dst[c, d].astype(F32)
        return total

    def quarter(q):
        def deep(kc, _):
            lhs = jnp.concatenate([work[16 * kc + c] for c in range(16)], axis=1)
            rhs = amps[pl.ds(pl.multiple_of(2048 * kc, 2048), 2048), 256 * q:256 * q + 256]
            y = jnp.dot(lhs, rhs, preferred_element_type=F32)
            for half in range(2):
                part = y[:, 128 * half:128 * half + 128]
                sums[half] = part + jnp.where(kc == 0, 0.0, sums[half])
            return 0

        lax.fori_loop(0, 2, deep, 0)
        for half in range(2):
            c = 2 * q + half
            for a in range(32):
                value = sums[half, pl.ds(a, 32, stride=32), :].astype(BF16)
                for h in range(2):
                    k = 2 * a + h
                    ku, kv = (k // 32 + k // 4) % 2 * 4 + k // 8 % 4, k % 8
                    one, two = (ku, kv) if c % 2 == 0 else (kv, ku)
                    send1[c, one, 16 * two:16 * two + 16, :] = value[16 * h:16 * h + 16]
            spread(0, c, send1, land1)

    def second(c):
        send2[c] = collect(0, c, send1, land1).astype(BF16).reshape(8, 16, 128)
        spread(1, c, send2, land2)

    quarter(0)
    quarter(1)
    quarter(2)
    second(0)
    second(1)
    quarter(3)
    for c in range(2, 8):
        second(c)
    for c in range(8):
        out[:, 128 * c:128 * c + 128] = collect(1, c, send2, land2)

    for copy in pending:
        copy.wait_send()


def on_device(raw_ints, metric, amplitudes, pair_list, occ_energy, vir_energy, window_ids):
    width = raw_ints.shape[1]
    raw_ca = jnp.transpose(raw_ints, (2, 1, 0)).reshape(2048, 128)
    raw_bd = jnp.transpose(raw_ints, (1, 2, 0)).reshape(2048, 128)
    amp = amplitudes.reshape(4096, 1024)
    vmem = lambda shape, kind: pltpu.VMEM(shape, kind)
    dma = pltpu.SemaphoreType.DMA
    summed = pl.pallas_call(
        ladder_kernel,
        out_shape=jax.ShapeDtypeStruct((16, 1024), F32),
        in_specs=[pl.BlockSpec(memory_space=pl.ANY)] * 4,
        out_specs=pl.BlockSpec(memory_space=pltpu.VMEM),
        scratch_shapes=[
            vmem((32, 1024, 128), BF16),
            vmem((8, 128, 1024), BF16),
            vmem((2048, 1024), F32),
            vmem((2048, 1024), BF16),
            vmem((1024, 2048), BF16),
            vmem((4096, 1024), BF16),
            vmem((2, 1024, 128), F32),
            vmem((8, 8, 128, 128), BF16),
            vmem((8, 7, 128, 128), BF16),
            vmem((8, 8, 16, 128), BF16),
            vmem((8, 7, 16, 128), BF16),
            dma((6,)), dma((8,)), dma((8,)),
            dma((3, 9)), dma((3, 9)), dma((3, 10)), dma((3, 10)),
            dma((2, 8, 7)), dma((2, 8, 7)),
        ],
        compiler_params=pltpu.CompilerParams(
            collective_id=0, has_side_effects=True, vmem_limit_bytes=60 * 2**20
        ),
        cost_estimate=pl.CostEstimate(flops=26 * 10**9, bytes_accessed=10 * 10**6, transcendentals=0),
    )(raw_ca, raw_bd, metric, amp)
    row_total = summed.shape[0]
    global_rows = lax.axis_index(("col", "dev")) * row_total + jnp.arange(row_total, dtype=jnp.int32)
    window_energy = select_energy(window_ids, vir_energy)
    energy_first = select_energy(global_rows // width, window_energy)
    energy_second = select_energy(global_rows % width, window_energy)
    energy_i = select_energy(pair_list[0], occ_energy)
    energy_j = select_energy(pair_list[1], occ_energy)
    denominator = (energy_i + energy_j)[None, :] - (energy_first + energy_second)[:, None]
    return summed / denominator


def solution(mesh):
    in_specs = (
        P("dev", None, "col"),
        P("dev", None),
        P("col", "dev", "ao"),
        P(None, "ao"),
        P(),
        P(),
        P(),
    )
    out_specs = P(("col", "dev"), "ao")
    return jax.shard_map(
        on_device, mesh=mesh, in_specs=in_specs, out_specs=out_specs, check_vma=False
    )
```

```python
import jax
import jax.numpy as jnp
from jax import lax
from jax.experimental import pallas as pl
from jax.experimental.pallas import tpu as pltpu
from jax.sharding import PartitionSpec as P

MESH = pl.DeviceIdType.MESH
F32, BF16 = jnp.float32, jnp.bfloat16
NT = (((1,), (1,)), ((), ()))

PARTNER, MINUS, PLUS, MINUS_P, PLUS_P, FAR_A, FAR_AP, FAR_B, FAR_BP = range(9)
OWN = 9


def select_energy(positions, table):
    labels = jnp.arange(table.shape[0], dtype=jnp.int32)
    return jnp.sum(jnp.where(positions[:, None] == labels[None, :], table[None, :], 0.0), axis=1)


def ladder_kernel(
    raw_bd, met, amp, out,
    raw, ladder, work, mbuf, acc_l, fac_l, fac_r, amps, sums, send1, land1, send2, land2,
    local_sem, deal_send, deal_recv, ag_send, ag_recv, rel_send, rel_recv, rs_send, rs_recv,
):
    i, j, o = lax.axis_index("col"), lax.axis_index("dev"), lax.axis_index("ao")
    flip = lambda g: lax.rem(g + 4, 8)
    ring = lambda g, step: (g // 4) * 4 + lax.rem(lax.rem(g, 4) + step, 4)
    along_dev = lambda g: (i, g, o)
    along_col = lambda g: (g, j, o)
    sibling = (i, j, 1 - o)
    u, v = lax.rem(i // 4 + j // 4, 2) * 4 + lax.rem(i, 4), j
    at = lambda u, v: (lax.rem(u // 4 + v // 4, 2) * 4 + lax.rem(u, 4), v, o)

    get_raw = pltpu.make_async_copy(raw_bd, raw, local_sem.at[0])
    get_raw.start()
    own_m = pltpu.make_async_copy(met, mbuf.at[j], local_sem.at[1])
    own_m.start()
    get_amps = pltpu.make_async_copy(amp, amps, local_sem.at[2])
    get_amps.start()

    barrier = pltpu.get_barrier_semaphore()

    def greet(device):
        pl.semaphore_signal(barrier, inc=1, device_id=device, device_id_type=MESH)

    for d in (1, 3):
        greet(along_col(ring(i, d)))
        greet(along_dev(ring(j, d)))
    greet(along_col(flip(i)))
    greet(along_dev(flip(j)))
    greet((flip(i), flip(j), o))
    greet(sibling)
    diagonal = i == j
    for k in range(8):
        @pl.when(jnp.logical_not(diagonal & (j == k)))
        def _():
            greet((j, k, o))

    get_raw.wait()
    sums[...] = jnp.zeros_like(sums)
    for half in range(2):
        for a in range(16):
            row = 1024 * half + 64 * a
            sums[half, 72 * a:72 * a + 64, :] = raw[row:row + 64, :].astype(F32)
    for c in range(64):
        rows = jnp.concatenate([sums[half, pl.ds(c, 16, stride=72), :] for half in range(2)], axis=0)
        work[2 * j + c // 32, 32 * (c % 32):32 * (c % 32) + 32, :] = rows.astype(BF16)
    pl.semaphore_wait(barrier, 16 - jnp.where(diagonal, 1, 0))

    pending = []

    def push(src, dst, send_sem, recv_sem, device):
        copy = pltpu.make_async_remote_copy(
            src_ref=src, dst_ref=dst, send_sem=send_sem, recv_sem=recv_sem,
            device_id=device, device_id_type=MESH,
        )
        copy.start()
        pending.append(copy)

    def landed(dst, recv_sem):
        pltpu.make_async_remote_copy(
            src_ref=dst, dst_ref=dst, send_sem=recv_sem, recv_sem=recv_sem,
            device_id=sibling, device_id_type=MESH,
        ).wait_recv()

    class Gather:
        def __init__(self, which, me, to, partner, half, part):
            self.which, self.me, self.half, self.part = which, me, half, part
            self.up, self.down = to(ring(me, 1)), to(ring(me, 3))
            self.partner = partner
            plus, minus, far = ring(me, 1), ring(me, 3), ring(me, 2)
            self.plus, self.minus, self.far = plus, minus, far
            self.place = {
                PARTNER: (flip(me), None), MINUS: (minus, None), PLUS: (plus, None),
                MINUS_P: (flip(minus), None), PLUS_P: (flip(plus), None),
                FAR_A: (far, 0), FAR_AP: (flip(far), 0), FAR_B: (far, 1), FAR_BP: (flip(far), 1),
            }

        def spot(self, kind, core):
            piece, quarter = self.place[kind]
            if quarter is None:
                return self.half(piece, core)
            return self.part(piece, core, quarter)

        def send(self, src, dst, kind, device):
            push(src, dst, ag_send.at[self.which, kind], ag_recv.at[self.which, kind], device)

        def send_own(self, src):
            dst = self.half(self.me, o)
            self.send(src, dst, MINUS, self.up)
            self.send(src, dst, PLUS, self.down)
            self.send(src, dst, PARTNER, self.partner)

        def arrive(self, *kinds):
            for kind in kinds:
                spot = self.spot(kind, o)
                landed(spot, ag_recv.at[self.which, kind])
                piece = self.place[kind][0]
                if kind == PARTNER:
                    self.send(spot, spot, MINUS_P, self.up)
                    self.send(spot, spot, PLUS_P, self.down)
                elif kind in (MINUS, MINUS_P):
                    first = self.part(piece, o, 0)
                    self.send(first, first, FAR_A if kind == MINUS else FAR_AP, self.up)
                elif kind in (PLUS, PLUS_P):
                    second = self.part(piece, o, 1)
                    self.send(second, second, FAR_B if kind == PLUS else FAR_BP, self.down)
                push(spot, spot, rel_send.at[self.which, kind], rel_recv.at[self.which, kind], sibling)

        def from_sibling(self, *kinds):
            for kind in kinds:
                landed(self.spot(kind, 1 - o), rel_recv.at[self.which, kind])

    left = Gather(
        0, j, along_dev, along_dev(flip(j)),
        lambda k, core: work.at[2 * k + core],
        lambda k, core, q: work.at[2 * k + core, pl.ds(512 * q, 512)],
    )
    right = Gather(
        1, i, along_col, along_col(flip(i)),
        lambda k, core: work.at[16 + 2 * k + core],
        lambda k, core, q: work.at[16 + 2 * k + core, pl.ds(512 * q, 512)],
    )
    fit = Gather(
        2, j, along_dev, (flip(i), flip(j), o),
        lambda k, core: mbuf.at[k, pl.ds(pl.multiple_of(64 * core, 64), 64)],
        lambda k, core, q: mbuf.at[k, pl.ds(pl.multiple_of(64 * core + 32 * q, 32), 32)],
    )

    fit.send_own(met.at[pl.ds(pl.multiple_of(64 * o, 64), 64)])
    chunk = lambda g: raw.at[pl.ds(pl.multiple_of(256 * g + 128 * o, 128), 128)]
    chunk_at = lambda g, k: work.at[16 + 2 * g + o, pl.ds(pl.multiple_of(128 * k, 128), 128)]
    for d in range(8):
        g = lax.rem(i + d, 8)

        @pl.when(jnp.logical_not(diagonal & (g == i)))
        def _():
            pltpu.make_async_remote_copy(
                src_ref=chunk(g), dst_ref=chunk_at(g, j), send_sem=deal_send.at[g],
                recv_sem=deal_recv.at[j], device_id=(g, i, o), device_id_type=MESH,
            ).start()

    @pl.when(diagonal)
    def _():
        here = pltpu.make_async_copy(chunk(i), chunk_at(i, j), local_sem.at[3])
        here.start()
        here.wait()

    fit.arrive(PARTNER, MINUS, PLUS)
    left.send_own(work.at[2 * j + o])
    for k in range(8):
        @pl.when(jnp.logical_not(diagonal & (j == k)))
        def _():
            landed(chunk_at(i, k), deal_recv.at[k])

    own_chunk = work.at[16 + 2 * i + o]
    right.send_own(own_chunk)
    push(own_chunk, own_chunk, rel_send.at[1, OWN], rel_recv.at[1, OWN], sibling)
    fit.arrive(MINUS_P, PLUS_P)
    left.arrive(PARTNER)
    right.arrive(PARTNER)
    fit.arrive(FAR_A, FAR_B, FAR_AP, FAR_BP)
    left.arrive(MINUS, PLUS, MINUS_P, PLUS_P)
    right.arrive(MINUS, PLUS)
    own_m.wait()
    fit.from_sibling(*range(9))

    def m_slice(k):
        return mbuf[:, :, pl.ds(pl.multiple_of(k * 128, 128), 128)].reshape(1024, 128)

    def fit_left(pieces, first=False, last=False):
        m = jnp.concatenate([m_slice(k) for k in pieces], axis=1)

        def body(n, _):
            rows = pl.ds(pl.multiple_of(n * 1024, 1024), 1024)
            x = jnp.concatenate([work[2 * k + n] for k in pieces], axis=1)
            y = lax.dot_general(x, m, NT, preferred_element_type=F32)
            if not first:
                y = y + acc_l[rows, :]
            if last:
                fac_l[rows, :] = y.astype(BF16)
            else:
                acc_l[rows, :] = y
            return 0

        lax.fori_loop(0, 2, body, 0)

    def fit_right(count, piece_of):
        def body(n, _):
            one = piece_of(n)
            two = flip(one)
            x = jnp.concatenate([
                jnp.concatenate([work[16 + 2 * g + h, 128 * k:128 * k + 128, :] for k in range(8)], axis=1)
                for g in (one, two) for h in range(2)
            ], axis=0)
            y = lax.dot_general(mbuf[...].reshape(1024, 1024), x, NT, preferred_element_type=F32).astype(BF16)
            fac_r[:, pl.ds(pl.multiple_of(256 * one, 256), 256)] = y[:, :256]
            fac_r[:, pl.ds(pl.multiple_of(256 * two, 256), 256)] = y[:, 256:]
            return 0

        lax.fori_loop(0, count, body, 0)

    def ladder_columns(pairs, piece_of):
        def body(n, _):
            g = piece_of(n // 2)
            g = lax.rem(g + 4 * lax.rem(n, 2), 8)
            cols = pl.ds(pl.multiple_of(256 * g, 256), 256)
            x = jnp.dot(fac_l[...], fac_r[:, cols], preferred_element_type=F32).astype(BF16)
            x = x.reshape(32, 2, 32, 256)
            even, odd = x[:, 0], x[:, 1]
            for n in range(4):
                lanes = slice(64 * n, 64 * n + 64)
                y = jnp.concatenate([even[:, :, lanes], odd[:, :, lanes]], axis=2)
                ladder[:, pl.ds(pl.multiple_of(128 * g + 32 * n, 32), 32), :] = y
            return 0

        lax.fori_loop(0, 2 * pairs, body, 0)

    left.from_sibling(PARTNER)
    fit_left([left.me, flip(left.me)], first=True)
    right.arrive(MINUS_P, PLUS_P)
    landed(work.at[16 + 2 * i + 1 - o], rel_recv.at[1, OWN])
    right.from_sibling(PARTNER)
    fit_right(1, lambda n: i)
    left.from_sibling(MINUS, MINUS_P, PLUS, PLUS_P)
    fit_left([left.minus, flip(left.minus), left.plus, flip(left.plus)])
    left.arrive(FAR_A, FAR_B, FAR_AP, FAR_BP)
    right.from_sibling(MINUS, MINUS_P, PLUS, PLUS_P)
    fit_right(2, lambda n: ring(i, 1 + 2 * n))
    left.from_sibling(FAR_A, FAR_B, FAR_AP, FAR_BP)
    fit_left([left.far, flip(left.far)], last=True)
    ladder_columns(1, lambda n: i)
    right.arrive(FAR_A, FAR_B, FAR_AP, FAR_BP)
    ladder_columns(2, lambda n: ring(i, 1 + 2 * n))
    right.from_sibling(FAR_A, FAR_B, FAR_AP, FAR_BP)
    fit_right(1, lambda n: right.far)
    ladder_columns(1, lambda n: right.far)
    get_amps.wait()

    def route(stage, c):
        if (c + stage) % 2 == 0:
            return u, lambda g: at(g, v)
        return v, lambda g: at(u, g)

    def spread(stage, c, src, dst):
        me, to = route(stage, c)
        for d in (1, 7, 4, 3, 5, 2, 6):
            peer = lax.rem(me + d, 8)
            push(src.at[c, peer], dst.at[c, d - 1], rs_send.at[stage, c, d - 1], rs_recv.at[stage, c, d - 1], to(peer))

    def collect(stage, c, src, dst):
        total = src[c, route(stage, c)[0]].astype(F32)
        for d in range(7):
            landed(dst.at[c, d], rs_recv.at[stage, c, d])
            total = total + dst[c, d].astype(F32)
        return total

    def quarter(q):
        def deep(kc, _):
            lhs = jnp.concatenate([ladder[16 * kc + c] for c in range(16)], axis=1)
            rhs = amps[pl.ds(pl.multiple_of(2048 * kc, 2048), 2048), 256 * q:256 * q + 256]
            y = jnp.dot(lhs, rhs, preferred_element_type=F32)
            for half in range(2):
                part = y[:, 128 * half:128 * half + 128]
                for b in range(32):
                    at_b = slice(40 * b, 40 * b + 32)
                    sums[half, at_b, :] = part[32 * b:32 * b + 32] + jnp.where(kc == 0, 0.0, sums[half, at_b, :])
            return 0

        lax.fori_loop(0, 2, deep, 0)
        for half in range(2):
            c = 2 * q + half
            for a in range(32):
                value = sums[half, pl.ds(a, 32, stride=40), :].astype(BF16)
                for h in range(2):
                    k = 2 * a + h
                    ku, kv = (k // 32 + k // 4) % 2 * 4 + k // 8 % 4, k % 8
                    one, two = (ku, kv) if c % 2 == 0 else (kv, ku)
                    send1[c, one, 16 * two:16 * two + 16, :] = value[16 * h:16 * h + 16]
            spread(0, c, send1, land1)

    def second(c):
        send2[c] = collect(0, c, send1, land1).astype(BF16).reshape(8, 16, 128)
        spread(1, c, send2, land2)

    quarter(0)
    quarter(1)
    quarter(2)
    second(0)
    second(1)
    quarter(3)
    for c in range(2, 8):
        second(c)
    for c in range(8):
        out[:, 128 * c:128 * c + 128] = collect(1, c, send2, land2)

    for copy in pending:
        copy.wait_send()
    for g in range(8):
        @pl.when(jnp.logical_not(diagonal & (g == i)))
        def _():
            pltpu.make_async_remote_copy(
                src_ref=chunk(g), dst_ref=chunk_at(g, j), send_sem=deal_send.at[g],
                recv_sem=deal_recv.at[j], device_id=(g, i, o), device_id_type=MESH,
            ).wait_send()


def on_device(raw_ints, metric, amplitudes, pair_list, occ_energy, vir_energy, window_ids):
    width = raw_ints.shape[1]
    raw_bd = jnp.transpose(raw_ints, (1, 2, 0)).reshape(2048, 128)
    amp = amplitudes.reshape(4096, 1024)
    vmem = lambda shape, kind: pltpu.VMEM(shape, kind)
    dma = pltpu.SemaphoreType.DMA
    summed = pl.pallas_call(
        ladder_kernel,
        out_shape=jax.ShapeDtypeStruct((16, 1024), F32),
        in_specs=[pl.BlockSpec(memory_space=pl.ANY)] * 3,
        out_specs=pl.BlockSpec(memory_space=pltpu.VMEM),
        scratch_shapes=[
            vmem((2048, 128), BF16),
            vmem((32, 1024, 128), BF16),
            vmem((32, 1024, 128), BF16),
            vmem((8, 128, 1024), BF16),
            vmem((2048, 1024), F32),
            vmem((2048, 1024), BF16),
            vmem((1024, 2048), BF16),
            vmem((4096, 1024), BF16),
            vmem((2, 1280, 128), F32),
            vmem((8, 8, 128, 128), BF16),
            vmem((8, 7, 128, 128), BF16),
            vmem((8, 8, 16, 128), BF16),
            vmem((8, 7, 16, 128), BF16),
            dma((6,)), dma((8,)), dma((8,)),
            dma((3, 9)), dma((3, 9)), dma((3, 10)), dma((3, 10)),
            dma((2, 8, 7)), dma((2, 8, 7)),
        ],
        compiler_params=pltpu.CompilerParams(
            collective_id=0, has_side_effects=True, vmem_limit_bytes=60 * 2**20
        ),
        cost_estimate=pl.CostEstimate(flops=26 * 10**9, bytes_accessed=10 * 10**6, transcendentals=0),
    )(raw_bd, metric, amp)
    row_total = summed.shape[0]
    global_rows = lax.axis_index(("col", "dev")) * row_total + jnp.arange(row_total, dtype=jnp.int32)
    window_energy = select_energy(window_ids, vir_energy)
    energy_first = select_energy(global_rows // width, window_energy)
    energy_second = select_energy(global_rows % width, window_energy)
    energy_i = select_energy(pair_list[0], occ_energy)
    energy_j = select_energy(pair_list[1], occ_energy)
    denominator = (energy_i + energy_j)[None, :] - (energy_first + energy_second)[:, None]
    return summed / denominator


def solution(mesh):
    in_specs = (
        P("dev", None, "col"),
        P("dev", None),
        P("col", "dev", "ao"),
        P(None, "ao"),
        P(),
        P(),
        P(),
    )
    out_specs = P(("col", "dev"), "ao")
    return jax.shard_map(
        on_device, mesh=mesh, in_specs=in_specs, out_specs=out_specs, check_vma=False
    )
```

```python
import jax
import jax.numpy as jnp
from jax import lax
from jax.experimental import pallas as pl
from jax.experimental.pallas import tpu as pltpu
from jax.sharding import PartitionSpec as P

MESH = pl.DeviceIdType.MESH
F32, BF16 = jnp.float32, jnp.bfloat16
NT = (((1,), (1,)), ((), ()))

PARTNER, MINUS, PLUS, MINUS_P, PLUS_P, FAR_A, FAR_AP, FAR_B, FAR_BP = range(9)
OWN = 9


def select_energy(positions, table):
    labels = jnp.arange(table.shape[0], dtype=jnp.int32)
    return jnp.sum(jnp.where(positions[:, None] == labels[None, :], table[None, :], 0.0), axis=1)


def ladder_kernel(
    raw_bd, met, amp, out,
    raw, ladder, work, mbuf, acc_l, fac_l, fac_r, amps, sums, send1, land1, send2, land2,
    local_sem, deal_send, deal_recv, ag_send, ag_recv, rel_send, rel_recv, rs_send, rs_recv,
):
    i, j, o = lax.axis_index("col"), lax.axis_index("dev"), lax.axis_index("ao")
    flip = lambda g: lax.rem(g + 4, 8)
    ring = lambda g, step: (g // 4) * 4 + lax.rem(lax.rem(g, 4) + step, 4)
    along_dev = lambda g: (i, g, o)
    along_col = lambda g: (g, j, o)
    sibling = (i, j, 1 - o)
    u, v = lax.rem(i // 4 + j // 4, 2) * 4 + lax.rem(i, 4), j
    at = lambda u, v: (lax.rem(u // 4 + v // 4, 2) * 4 + lax.rem(u, 4), v, o)

    get_raw = pltpu.make_async_copy(raw_bd, raw, local_sem.at[0])
    get_raw.start()
    own_m = pltpu.make_async_copy(met, mbuf.at[j], local_sem.at[1])
    own_m.start()
    get_amps = pltpu.make_async_copy(amp, amps, local_sem.at[2])
    get_amps.start()

    barrier = pltpu.get_barrier_semaphore()

    def greet(device):
        pl.semaphore_signal(barrier, inc=1, device_id=device, device_id_type=MESH)

    for d in (1, 3):
        greet(along_col(ring(i, d)))
        greet(along_dev(ring(j, d)))
    greet(along_col(flip(i)))
    greet(along_dev(flip(j)))
    greet((flip(i), flip(j), o))
    greet(sibling)
    diagonal = i == j
    for k in range(8):
        @pl.when(jnp.logical_not(diagonal & (j == k)))
        def _():
            greet((j, k, o))

    get_raw.wait()
    sums[...] = jnp.zeros_like(sums)
    for half in range(2):
        for a in range(16):
            row = 1024 * half + 64 * a
            sums[half, 72 * a:72 * a + 64, :] = raw[row:row + 64, :].astype(F32)
    for c in range(64):
        rows = jnp.concatenate([sums[half, pl.ds(c, 16, stride=72), :] for half in range(2)], axis=0)
        work[2 * j + c // 32, 32 * (c % 32):32 * (c % 32) + 32, :] = rows.astype(BF16)
    pl.semaphore_wait(barrier, 16 - jnp.where(diagonal, 1, 0))

    pending = []

    def push(src, dst, send_sem, recv_sem, device):
        copy = pltpu.make_async_remote_copy(
            src_ref=src, dst_ref=dst, send_sem=send_sem, recv_sem=recv_sem,
            device_id=device, device_id_type=MESH,
        )
        copy.start()
        pending.append(copy)

    def landed(dst, recv_sem):
        pltpu.make_async_remote_copy(
            src_ref=dst, dst_ref=dst, send_sem=recv_sem, recv_sem=recv_sem,
            device_id=sibling, device_id_type=MESH,
        ).wait_recv()

    class Gather:
        def __init__(self, which, me, to, partner, half, part):
            self.which, self.me, self.half, self.part = which, me, half, part
            self.up, self.down = to(ring(me, 1)), to(ring(me, 3))
            self.partner = partner
            plus, minus, far = ring(me, 1), ring(me, 3), ring(me, 2)
            self.plus, self.minus, self.far = plus, minus, far
            self.place = {
                PARTNER: (flip(me), None), MINUS: (minus, None), PLUS: (plus, None),
                MINUS_P: (flip(minus), None), PLUS_P: (flip(plus), None),
                FAR_A: (far, 0), FAR_AP: (flip(far), 0), FAR_B: (far, 1), FAR_BP: (flip(far), 1),
            }

        def spot(self, kind, core):
            piece, quarter = self.place[kind]
            if quarter is None:
                return self.half(piece, core)
            return self.part(piece, core, quarter)

        def send(self, src, dst, kind, device):
            push(src, dst, ag_send.at[self.which, kind], ag_recv.at[self.which, kind], device)

        def send_own(self, src):
            dst = self.half(self.me, o)
            self.send(src, dst, MINUS, self.up)
            self.send(src, dst, PLUS, self.down)
            self.send(src, dst, PARTNER, self.partner)

        def arrive(self, *kinds):
            for kind in kinds:
                spot = self.spot(kind, o)
                landed(spot, ag_recv.at[self.which, kind])
                piece = self.place[kind][0]
                if kind == PARTNER:
                    self.send(spot, spot, MINUS_P, self.up)
                    self.send(spot, spot, PLUS_P, self.down)
                elif kind in (MINUS, MINUS_P):
                    first = self.part(piece, o, 0)
                    self.send(first, first, FAR_A if kind == MINUS else FAR_AP, self.up)
                elif kind in (PLUS, PLUS_P):
                    second = self.part(piece, o, 1)
                    self.send(second, second, FAR_B if kind == PLUS else FAR_BP, self.down)
                push(spot, spot, rel_send.at[self.which, kind], rel_recv.at[self.which, kind], sibling)

        def from_sibling(self, *kinds):
            for kind in kinds:
                landed(self.spot(kind, 1 - o), rel_recv.at[self.which, kind])

    left = Gather(
        0, j, along_dev, along_dev(flip(j)),
        lambda k, core: work.at[2 * k + core],
        lambda k, core, q: work.at[2 * k + core, pl.ds(512 * q, 512)],
    )
    right = Gather(
        1, i, along_col, along_col(flip(i)),
        lambda k, core: work.at[16 + 2 * k + core],
        lambda k, core, q: work.at[16 + 2 * k + core, pl.ds(512 * q, 512)],
    )
    fit = Gather(
        2, j, along_dev, (flip(i), flip(j), o),
        lambda k, core: mbuf.at[k, pl.ds(pl.multiple_of(64 * core, 64), 64)],
        lambda k, core, q: mbuf.at[k, pl.ds(pl.multiple_of(64 * core + 32 * q, 32), 32)],
    )

    chunk = lambda g: raw.at[pl.ds(pl.multiple_of(256 * g + 128 * o, 128), 128)]
    chunk_at = lambda g, k: work.at[16 + 2 * g + o, pl.ds(pl.multiple_of(128 * k, 128), 128)]
    for d in range(8):
        g = lax.rem(i + d, 8)

        @pl.when(jnp.logical_not(diagonal & (g == i)))
        def _():
            pltpu.make_async_remote_copy(
                src_ref=chunk(g), dst_ref=chunk_at(g, j), send_sem=deal_send.at[g],
                recv_sem=deal_recv.at[j], device_id=(g, i, o), device_id_type=MESH,
            ).start()

    fit.send_own(met.at[pl.ds(pl.multiple_of(64 * o, 64), 64)])

    @pl.when(diagonal)
    def _():
        here = pltpu.make_async_copy(chunk(i), chunk_at(i, j), local_sem.at[3])
        here.start()
        here.wait()

    fit.arrive(PARTNER, MINUS, PLUS)
    left.send_own(work.at[2 * j + o])
    for k in range(8):
        @pl.when(jnp.logical_not(diagonal & (j == k)))
        def _():
            landed(chunk_at(i, k), deal_recv.at[k])

    own_chunk = work.at[16 + 2 * i + o]
    right.send_own(own_chunk)
    push(own_chunk, own_chunk, rel_send.at[1, OWN], rel_recv.at[1, OWN], sibling)
    fit.arrive(MINUS_P, PLUS_P)
    left.arrive(PARTNER)
    right.arrive(PARTNER)
    fit.arrive(FAR_A, FAR_B, FAR_AP, FAR_BP)
    left.arrive(MINUS, PLUS, MINUS_P, PLUS_P)
    right.arrive(MINUS, PLUS)
    own_m.wait()
    fit.from_sibling(*range(9))

    def m_slice(k):
        return mbuf[:, :, pl.ds(pl.multiple_of(k * 128, 128), 128)].reshape(1024, 128)

    def fit_left(pieces, first=False, last=False):
        m = jnp.concatenate([m_slice(k) for k in pieces], axis=1)

        def body(n, _):
            rows = pl.ds(pl.multiple_of(n * 1024, 1024), 1024)
            x = jnp.concatenate([work[2 * k + n] for k in pieces], axis=1)
            y = lax.dot_general(x, m, NT, preferred_element_type=F32)
            if not first:
                y = y + acc_l[rows, :]
            if last:
                fac_l[rows, :] = y.astype(BF16)
            else:
                acc_l[rows, :] = y
            return 0

        lax.fori_loop(0, 2, body, 0)

    def fit_right(count, piece_of):
        def body(n, _):
            one = piece_of(n)
            two = flip(one)
            x = jnp.concatenate([
                jnp.concatenate([work[16 + 2 * g + h, 128 * k:128 * k + 128, :] for k in range(8)], axis=1)
                for g in (one, two) for h in range(2)
            ], axis=0)
            y = lax.dot_general(mbuf[...].reshape(1024, 1024), x, NT, preferred_element_type=F32).astype(BF16)
            fac_r[:, pl.ds(pl.multiple_of(256 * one, 256), 256)] = y[:, :256]
            fac_r[:, pl.ds(pl.multiple_of(256 * two, 256), 256)] = y[:, 256:]
            return 0

        lax.fori_loop(0, count, body, 0)

    def ladder_columns(pairs, piece_of):
        def body(n, _):
            g = piece_of(n // 2)
            g = lax.rem(g + 4 * lax.rem(n, 2), 8)
            cols = pl.ds(pl.multiple_of(256 * g, 256), 256)
            x = jnp.dot(fac_l[...], fac_r[:, cols], preferred_element_type=F32).astype(BF16)
            x = x.reshape(32, 2, 32, 256)
            even, odd = x[:, 0], x[:, 1]
            low = lax.broadcasted_iota(jnp.int32, (32, 32, 128), 2) < 64
            for n in range(2):
                x0, x1 = even[:, :, 128 * n:128 * n + 128], odd[:, :, 128 * n:128 * n + 128]
                mixed = jnp.where(low, x1, x0)
                mixed = jnp.concatenate([mixed[:, :, 64:], mixed[:, :, :64]], axis=2)
                at_b = pl.multiple_of(128 * g + 64 * n, 64)
                ladder[:, pl.ds(at_b, 32), :] = jnp.where(low, x0, mixed)
                ladder[:, pl.ds(at_b + 32, 32), :] = jnp.where(low, mixed, x1)
            return 0

        lax.fori_loop(0, 2 * pairs, body, 0)

    left.from_sibling(PARTNER)
    fit_left([left.me, flip(left.me)], first=True)
    right.arrive(MINUS_P, PLUS_P)
    landed(work.at[16 + 2 * i + 1 - o], rel_recv.at[1, OWN])
    right.from_sibling(PARTNER)
    fit_right(1, lambda n: i)
    left.from_sibling(MINUS, MINUS_P, PLUS, PLUS_P)
    fit_left([left.minus, flip(left.minus), left.plus, flip(left.plus)])
    left.arrive(FAR_A, FAR_B, FAR_AP, FAR_BP)
    right.from_sibling(MINUS, MINUS_P, PLUS, PLUS_P)
    fit_right(2, lambda n: ring(i, 1 + 2 * n))
    left.from_sibling(FAR_A, FAR_B, FAR_AP, FAR_BP)
    fit_left([left.far, flip(left.far)], last=True)
    ladder_columns(1, lambda n: i)
    right.arrive(FAR_A, FAR_B, FAR_AP, FAR_BP)
    ladder_columns(2, lambda n: ring(i, 1 + 2 * n))
    right.from_sibling(FAR_A, FAR_B, FAR_AP, FAR_BP)
    fit_right(1, lambda n: right.far)
    ladder_columns(1, lambda n: right.far)
    get_amps.wait()

    def route(stage, c):
        if (c + stage) % 2 == 0:
            return u, lambda g: at(g, v)
        return v, lambda g: at(u, g)

    def spread(stage, c, src, dst):
        me, to = route(stage, c)
        for d in (1, 7, 4, 3, 5, 2, 6):
            peer = lax.rem(me + d, 8)
            push(src.at[c, peer], dst.at[c, d - 1], rs_send.at[stage, c, d - 1], rs_recv.at[stage, c, d - 1], to(peer))

    def collect(stage, c, src, dst):
        total = src[c, route(stage, c)[0]].astype(F32)
        for d in range(7):
            landed(dst.at[c, d], rs_recv.at[stage, c, d])
            total = total + dst[c, d].astype(F32)
        return total

    def quarter(q):
        def deep(kc, _):
            lhs = jnp.concatenate([ladder[16 * kc + c] for c in range(16)], axis=1)
            rhs = amps[pl.ds(pl.multiple_of(2048 * kc, 2048), 2048), 256 * q:256 * q + 256]
            y = jnp.dot(lhs, rhs, preferred_element_type=F32)
            for half in range(2):
                part = y[:, 128 * half:128 * half + 128]
                for b in range(32):
                    at_b = slice(40 * b, 40 * b + 32)
                    sums[half, at_b, :] = part[32 * b:32 * b + 32] + jnp.where(kc == 0, 0.0, sums[half, at_b, :])
            return 0

        lax.fori_loop(0, 2, deep, 0)
        for half in range(2):
            c = 2 * q + half
            for a in range(32):
                value = sums[half, pl.ds(a, 32, stride=40), :].astype(BF16)
                for h in range(2):
                    k = 2 * a + h
                    ku, kv = (k // 32 + k // 4) % 2 * 4 + k // 8 % 4, k % 8
                    one, two = (ku, kv) if c % 2 == 0 else (kv, ku)
                    send1[c, one, 16 * two:16 * two + 16, :] = value[16 * h:16 * h + 16]
            spread(0, c, send1, land1)

    def second(c):
        send2[c] = collect(0, c, send1, land1).astype(BF16).reshape(8, 16, 128)
        spread(1, c, send2, land2)

    quarter(0)
    quarter(1)
    quarter(2)
    second(0)
    second(1)
    quarter(3)
    for c in range(2, 8):
        second(c)
    for c in range(8):
        out[:, 128 * c:128 * c + 128] = collect(1, c, send2, land2)

    for copy in pending:
        copy.wait_send()
    for g in range(8):
        @pl.when(jnp.logical_not(diagonal & (g == i)))
        def _():
            pltpu.make_async_remote_copy(
                src_ref=chunk(g), dst_ref=chunk_at(g, j), send_sem=deal_send.at[g],
                recv_sem=deal_recv.at[j], device_id=(g, i, o), device_id_type=MESH,
            ).wait_send()


def on_device(raw_ints, metric, amplitudes, pair_list, occ_energy, vir_energy, window_ids):
    width = raw_ints.shape[1]
    raw_bd = jnp.transpose(raw_ints, (1, 2, 0)).reshape(2048, 128)
    amp = amplitudes.reshape(4096, 1024)
    vmem = lambda shape, kind: pltpu.VMEM(shape, kind)
    dma = pltpu.SemaphoreType.DMA
    summed = pl.pallas_call(
        ladder_kernel,
        out_shape=jax.ShapeDtypeStruct((16, 1024), F32),
        in_specs=[pl.BlockSpec(memory_space=pl.ANY)] * 3,
        out_specs=pl.BlockSpec(memory_space=pltpu.VMEM),
        scratch_shapes=[
            vmem((2048, 128), BF16),
            vmem((32, 1024, 128), BF16),
            vmem((32, 1024, 128), BF16),
            vmem((8, 128, 1024), BF16),
            vmem((2048, 1024), F32),
            vmem((2048, 1024), BF16),
            vmem((1024, 2048), BF16),
            vmem((4096, 1024), BF16),
            vmem((2, 1280, 128), F32),
            vmem((8, 8, 128, 128), BF16),
            vmem((8, 7, 128, 128), BF16),
            vmem((8, 8, 16, 128), BF16),
            vmem((8, 7, 16, 128), BF16),
            dma((6,)), dma((8,)), dma((8,)),
            dma((3, 9)), dma((3, 9)), dma((3, 10)), dma((3, 10)),
            dma((2, 8, 7)), dma((2, 8, 7)),
        ],
        compiler_params=pltpu.CompilerParams(
            collective_id=0, has_side_effects=True, vmem_limit_bytes=60 * 2**20
        ),
        cost_estimate=pl.CostEstimate(flops=26 * 10**9, bytes_accessed=10 * 10**6, transcendentals=0),
    )(raw_bd, metric, amp)
    row_total = summed.shape[0]
    global_rows = lax.axis_index(("col", "dev")) * row_total + jnp.arange(row_total, dtype=jnp.int32)
    window_energy = select_energy(window_ids, vir_energy)
    energy_first = select_energy(global_rows // width, window_energy)
    energy_second = select_energy(global_rows % width, window_energy)
    energy_i = select_energy(pair_list[0], occ_energy)
    energy_j = select_energy(pair_list[1], occ_energy)
    denominator = (energy_i + energy_j)[None, :] - (energy_first + energy_second)[:, None]
    return summed / denominator


def solution(mesh):
    in_specs = (
        P("dev", None, "col"),
        P("dev", None),
        P("col", "dev", "ao"),
        P(None, "ao"),
        P(),
        P(),
        P(),
    )
    out_specs = P(("col", "dev"), "ao")
    return jax.shard_map(
        on_device, mesh=mesh, in_specs=in_specs, out_specs=out_specs, check_vma=False
    )
```
